32 devices in a mesh: rows: 8 (over z, y), bands: 4 (over x, core).
Axes of the slice: x: 2, y: 2, z: 4, core: 2. Of those that a mesh axis runs over, the one named last changes fastest.
Arguments:
- vectors: float32 [8192, 1024], P('rows', 'bands'), may hold values from -6 to 6
- local_blocks: float32 [64, 6, 128, 128], P('rows'), may hold values from -0.078125 to 0.078125
- local_cols: int32 [64, 6], P('rows'), may hold values from 0 to 7
- coupling_blocks: float32 [3, 64, 2, 128, 128], P(None, 'rows'), may hold values from -0.078125 to 0.078125
- coupling_cols: int32 [3, 64, 2], replicated, may hold values from 0 to 7
- partners: int32 [3, 8], replicated, may hold values from 0 to 7, as said below
- bounds: float32 [3], replicated, may hold values from -2.8 to 2.8, as said below
- rotation: float32 [1024, 1024], replicated, may hold values from -1 to 1
Outputs:
- rotated: float32 [8192, 1024], P('rows', 'bands')
The draws below stay inside these ranges and needn't reach their ends.
Inputs may be any that keep to these rules, and one draw needn't show every extreme that they name: For each colour c there is a bit number b_c, with the three b_c distinct, such that partners[c, i] = i XOR 2 ** b_c for every row shard i. `local_cols`: local block columns count inside the row shard itself. `coupling_cols`: coupling block columns count inside the partner shard of that colour. bounds[0] < bounds[1] < bounds[2].
All inputs are finite; a program needn't handle non-finite values.
Results may differ from the reference program's by a relative error of at most 0.0003.
Values sent between devices are 32-bit elements; how exact they have to be, the bound alone decides.
No kernel may reach another device: no remote copies, remote signals or barrier semaphores. Data moves between devices by JAX's collectives and lax.ppermute only.
A program may use at most 128 MiB of HBM per device.

```python
import jax
import jax.numpy as jnp
from jax import lax

BLK = 128
KL = 6
KC = 2
NB = 1024
ROWS_DEV = 1024
TOTAL_ROWS = 8192
NBLK = 64
N_ROWS = 8


def draw_partners(key, part):
    bit_total = N_ROWS.bit_length() - 1
    chosen = jax.random.permutation(jax.random.fold_in(key, 11), bit_total)[:3].astype(jnp.int32)
    masks = jnp.left_shift(jnp.ones((3,), jnp.int32), chosen)
    shard_ids = jnp.arange(N_ROWS, dtype=jnp.int32)
    return jnp.bitwise_xor(shard_ids[None, :], masks[:, None]).astype(jnp.int32)


def draw_bounds(key, part):
    sub_keys = jax.random.split(jax.random.fold_in(key, 5), 3)
    lowest = jax.random.uniform(sub_keys[0], (), jnp.float32, -2.8, -2.3)
    lower = jax.random.uniform(sub_keys[1], (), jnp.float32, -1.2, -0.6)
    upper = jax.random.uniform(sub_keys[2], (), jnp.float32, 2.2, 2.8)
    return jnp.stack([lowest, lower, upper])


def draw_rotation(key, part):
    inner_key = jax.random.fold_in(key, 7)
    base = jax.random.normal(inner_key, (NB, NB), jnp.float32)
    orthogonal, upper_part = jnp.linalg.qr(base)
    return orthogonal.astype(jnp.float32)


def set_ends(entries, key, least, top_value):
    place = [jax.random.randint(jax.random.fold_in(key, axis), (), 0, length) for axis, length in enumerate(entries.shape)]
    main_axis = entries.shape.index(max(entries.shape))
    next_to = place[:main_axis] + [(place[main_axis] + 1) % entries.shape[main_axis]] + place[main_axis + 1:]
    return entries.at[tuple(place)].set(least).at[tuple(next_to)].set(top_value)


def levels(rng, shape, pieces, low, high):
    loudness = 1.0
    for position, blocks in pieces:
        heights = jax.random.uniform(jax.random.fold_in(jax.random.fold_in(rng, 6), position), (blocks,), jnp.float32, low / len(pieces), high / len(pieces))
        loudness = loudness * jnp.repeat(jnp.exp(heights), shape[position] // blocks).reshape((-1,) + (1,) * (len(shape) - 1 - position))
    return loudness


def centred(stream_key, dims, deviation, most, pieces=(), kind=jnp.bfloat16):
    level = levels(stream_key, dims, pieces, -0.22, 0.18) if pieces else 1.0
    values = jax.random.normal(stream_key, dims, jnp.float32) * deviation * level
    return jnp.minimum(jnp.maximum(values, -most), most).astype(kind)


def setup_inputs(seed: int = 0) -> dict:
    keys = jax.random.split(jax.random.key(seed), 9)
    return {
        "vectors": centred(keys[0], (TOTAL_ROWS, NB), 1.0, 6.0, ((0, 8), (1, 4)), jnp.float32),
        "local_blocks": centred(keys[1], (NBLK, KL, BLK, BLK), (4 * BLK * (KL + 3 * KC)) ** -0.5, 0.078125, ((0, 8),), jnp.float32),
        "local_cols": set_ends(jax.random.randint(keys[2], (NBLK, KL), 0, ROWS_DEV // BLK), jax.random.fold_in(keys[2], 1), 0, (ROWS_DEV // BLK) - 1).astype(jnp.int32),
        "coupling_blocks": centred(keys[3], (3, NBLK, KC, BLK, BLK), (4 * BLK * (KL + 3 * KC)) ** -0.5, 0.078125, ((1, 8),), jnp.float32),
        "coupling_cols": set_ends(jax.random.randint(keys[4], (3, NBLK, KC), 0, ROWS_DEV // BLK), jax.random.fold_in(keys[4], 1), 0, (ROWS_DEV // BLK) - 1).astype(jnp.int32),
        "partners": draw_partners(jax.random.fold_in(keys[8], 71), 0),
        "bounds": draw_bounds(jax.random.fold_in(keys[8], 71), 0),
        "rotation": draw_rotation(jax.random.fold_in(keys[8], 71), 0),
    }


precise = lax.Precision.HIGHEST

def forward(blocks, block_cols, source):
    picked = jnp.take(source, block_cols, axis=0)
    return jnp.einsum('akij,akjw->aiw', blocks, picked, precision=precise)

def backward(blocks, block_cols, source, block_count):
    products = jnp.einsum('akij,aiw->akjw', blocks, source, precision=precise)
    targets = jnp.arange(block_count, dtype=jnp.int32)
    onehot = (block_cols[:, :, None] == targets[None, None, :]).astype(jnp.float32)
    return jnp.einsum('akc,akjw->cjw', onehot, products, precision=precise)

def apply_hamiltonian(current, local_blocks, local_cols, coupling_blocks, coupling_cols, partners):
    shard_count = partners.shape[1]
    block_count = ROWS_DEV // BLK
    shards_view = current.reshape(shard_count, block_count, BLK, NB)
    local_view = local_blocks.reshape(shard_count, block_count, KL, BLK, BLK)
    local_index = local_cols.reshape(shard_count, block_count, KL)
    couple_view = coupling_blocks.reshape(3, shard_count, block_count, KC, BLK, BLK)
    couple_index = coupling_cols.reshape(3, shard_count, block_count, KC)

    def one_shard(shard):
        own = shards_view[shard]
        result = forward(local_view[shard], local_index[shard], own)
        result = result + backward(local_view[shard], local_index[shard], own, block_count)
        for colour in range(3):
            mate = partners[colour, shard]
            mate_field = shards_view[mate]
            result = result + forward(couple_view[colour, shard], couple_index[colour, shard], mate_field)
            result = result + backward(couple_view[colour, mate], couple_index[colour, mate], mate_field, block_count)
        return result
    outcome = lax.map(one_shard, jnp.arange(shard_count, dtype=jnp.int32))
    return outcome.reshape(current.shape)

def reference(vectors, local_blocks, local_cols, coupling_blocks, coupling_cols, partners, bounds, rotation):
    lowest, lower, upper = (bounds[0], bounds[1], bounds[2])
    half_width = (upper - lower) / 2.0
    centre = (upper + lower) / 2.0
    sigma_one = half_width / (lowest - centre)
    sigma_two = 1.0 / (2.0 / sigma_one - sigma_one)

    def apply_field(current):
        return apply_hamiltonian(current, local_blocks, local_cols, coupling_blocks, coupling_cols, partners)
    filtered = (apply_field(vectors) - centre * vectors) * (sigma_one / half_width)
    second = (apply_field(filtered) - centre * filtered) * (2.0 * sigma_two / half_width) - sigma_one * sigma_two * vectors
    return jnp.dot(second.astype(jnp.float32), rotation.astype(jnp.float32), precision=precise, preferred_element_type=jnp.float32)
```

```python
import functools

import jax
import jax.numpy as jnp
from jax import lax
from jax.experimental import pallas as pl
from jax.experimental.pallas import tpu as pltpu
from jax.sharding import PartitionSpec as P

f32 = jnp.float32
bf16 = jnp.bfloat16
ANY = pl.BlockSpec(memory_space=pl.ANY)
VMEM = pl.BlockSpec(memory_space=pltpu.VMEM)
SMEM = pl.BlockSpec(memory_space=pltpu.SMEM)
PARAMS = pltpu.CompilerParams(vmem_limit_bytes=44 * 1024 * 1024)


def split(x):
    hi = x.astype(bf16)
    return hi, (x - hi.astype(f32)).astype(bf16)


def dot(a, b):
    return jnp.dot(a, b, preferred_element_type=f32)


def rotate_kernel(pick_ref, own_ref, mate_ref, r_own_ref, r_mate_ref, *outs):
    total = None
    for v_ref, r_ref in ((own_ref, r_own_ref), (mate_ref, r_mate_ref)):
        v_hi, v_lo = split(v_ref[...])
        r_hi, r_lo = split(r_ref[...])
        part = dot(v_hi, r_hi) + dot(v_lo, r_hi) + dot(v_hi, r_lo)
        total = part if total is None else total + part
    halves = len(outs)
    rows = outs[0][0].shape[0] if isinstance(outs[0], tuple) else outs[0].shape[0]
    width = outs[0].shape[1]
    per_col = total.shape[0] // rows
    for n in range(halves):
        c, r = n // per_col, n % per_col
        outs[n][...] = total[r * rows:(r + 1) * rows, c * width:(c + 1) * width]


def rotate(own, mate, rotation, pick, chunk_rows, width):
    rows, band = own.shape
    count = (rows // chunk_rows) * (band // width)
    full = pl.BlockSpec((rows, band), lambda i, p: (0, 0))
    return pl.pallas_call(
        rotate_kernel,
        grid_spec=pltpu.PrefetchScalarGridSpec(
            num_scalar_prefetch=1,
            grid=(1,),
            in_specs=[
                full,
                full,
                pl.BlockSpec((band, band), lambda i, p: (p[0], p[2])),
                pl.BlockSpec((band, band), lambda i, p: (p[1], p[2])),
            ],
            out_specs=[pl.BlockSpec((chunk_rows, width), lambda i, p: (0, 0))] * count,
        ),
        out_shape=[jax.ShapeDtypeStruct((chunk_rows, width), f32)] * count,
        compiler_params=PARAMS,
        cost_estimate=pl.CostEstimate(
            flops=6 * 2 * rows * band * band, bytes_accessed=3 * rows * band * 4, transcendentals=0
        ),
        name="rotate",
    )(pick, own, mate, rotation, rotation)


def write_parts(acc, hi_ref, lo_ref):
    count, _, size, _ = acc.shape

    def one(i, carry):
        for j in range(count):
            hi, lo = split(acc[i, j])
            rows = pl.ds(pl.multiple_of(i * size, size), size)
            hi_ref[rows, j * size:(j + 1) * size] = hi
            lo_ref[rows, j * size:(j + 1) * size] = lo
        return carry

    lax.fori_loop(0, count, one, 0)


def local_kernel(cols_ref, bounds_ref, blocks_ref, hi_ref, lo_ref, acc):
    count, _, size, _ = acc.shape
    stored = blocks_ref.shape[1]
    acc[...] = jnp.zeros_like(acc)
    centre = (bounds_ref[2] + bounds_ref[1]) / 2.0
    eye = lax.broadcasted_iota(jnp.int32, (size, size), 0) == lax.broadcasted_iota(
        jnp.int32, (size, size), 1
    )
    shift = jnp.where(eye, -centre, 0.0).astype(f32)
    for i in range(count):
        acc[i, i] = shift

    def one(a, carry):
        for k in range(stored):
            block = blocks_ref[a, k]
            col = cols_ref[a, k]
            acc[a, col] += block
            acc[col, a] += block.T
        return carry

    lax.fori_loop(0, count, one, 0)
    write_parts(acc, hi_ref, lo_ref)


def build_local(blocks, cols, bounds):
    count, stored, size, _ = blocks.shape
    rows = count * size
    return pl.pallas_call(
        local_kernel,
        in_specs=[SMEM, SMEM, VMEM],
        out_specs=[VMEM, VMEM],
        out_shape=[jax.ShapeDtypeStruct((rows, rows), bf16)] * 2,
        scratch_shapes=[pltpu.VMEM((count, count, size, size), f32)],
        compiler_params=PARAMS,
        cost_estimate=pl.CostEstimate(
            flops=rows * rows, bytes_accessed=rows * rows * 12, transcendentals=0
        ),
        name="build_local",
    )(cols, bounds, blocks)


def couple_kernel(pieces, meta_ref, own_cols_ref, mate_cols_ref, blocks_ref, *rest):
    piece_refs, (hi_ref, lo_ref, acc) = rest[:pieces], rest[pieces:]
    count = acc.shape[0]
    stored = blocks_ref.shape[2]
    acc[...] = jnp.zeros_like(acc)

    def own(a, carry):
        for k in range(stored):
            acc[a, own_cols_ref[a, k]] += blocks_ref[0, a, k]
        return carry

    lax.fori_loop(0, count, own, 0)
    for n, piece in enumerate(piece_refs):
        for i in range(piece.shape[0]):
            a = meta_ref[1 + n] + i
            for k in range(stored):
                acc[mate_cols_ref[a, k], a] += piece[i, k].T
    write_parts(acc, hi_ref, lo_ref)


def build_couple(meta, own_cols, mate_cols, coupling_blocks, pieces):
    _, count, stored, size, _ = coupling_blocks.shape
    rows = count * size
    whole = pl.BlockSpec((rows, rows), lambda i, *_: (0, 0))
    return pl.pallas_call(
        functools.partial(couple_kernel, len(pieces)),
        grid_spec=pltpu.PrefetchScalarGridSpec(
            num_scalar_prefetch=3,
            grid=(1,),
            in_specs=[pl.BlockSpec((1, count, stored, size, size), lambda i, m, *_: (m[0], 0, 0, 0, 0))]
            + [pl.BlockSpec(p.shape, lambda i, *_: (0, 0, 0, 0)) for p in pieces],
            out_specs=[whole, whole],
            scratch_shapes=[pltpu.VMEM((count, count, size, size), f32)],
        ),
        out_shape=[jax.ShapeDtypeStruct((rows, rows), bf16)] * 2,
        compiler_params=PARAMS,
        cost_estimate=pl.CostEstimate(
            flops=rows * rows, bytes_accessed=rows * rows * 8, transcendentals=0
        ),
        name="build_couple",
    )(meta, own_cols, mate_cols, coupling_blocks, *pieces)


def apply_kernel(chunk_counts, has_base, column, scale_ref, *refs):
    refs = list(refs)
    mats = []
    for chunks in chunk_counts:
        hi, lo = refs.pop(0), refs.pop(0)
        mats.append((hi, lo, [refs.pop(0) for _ in range(chunks)]))
    base = [refs.pop(0) for _ in range(has_base)]
    if column is not None and column > 0:
        refs.pop(0)
    out_ref, hi_buf, lo_buf, u_buf, base_buf, w_buf, acc, sems, out_sem = refs
    copies = []
    n = 0
    for m, (hi, lo, chunks) in enumerate(mats):
        mine = [(hi, hi_buf.at[m]), (lo, lo_buf.at[m])]
        at = 0
        for chunk in chunks:
            mine.append((chunk, u_buf.at[m, at:at + chunk.shape[0]]))
            at += chunk.shape[0]
        group = []
        for src, dst in mine:
            group.append(pltpu.make_async_copy(src, dst, sems.at[n]))
            n += 1
        copies.append(group)
    base_group = []
    at = 0
    for chunk in base:
        base_group.append(
            pltpu.make_async_copy(chunk, base_buf.at[at:at + chunk.shape[0]], sems.at[n])
        )
        at += chunk.shape[0]
        n += 1
    for group in copies + [base_group]:
        for c in group:
            c.start()
    rows, width = acc.shape
    for m in range(len(mats)):
        for c in copies[m]:
            c.wait()
        u_hi, u_lo = split(u_buf[m])
        w_buf[:, :width] = u_hi
        w_buf[:, width:] = u_lo
        both = dot(hi_buf[m], w_buf[...])
        part = both[:, :width] + both[:, width:] + dot(lo_buf[m], w_buf[:, :width])
        if m == 0:
            acc[...] = part
        else:
            acc[...] += part
    for c in base_group:
        c.wait()
    result = acc[...] * scale_ref[0]
    if base_group:
        result = result + base_buf[...] * scale_ref[1]
    if column is None:
        out_ref[...] = result
    else:
        acc[...] = result
        c = pltpu.make_async_copy(acc, out_ref.at[:, column:column + width], out_sem)
        c.start()
        c.wait()


def apply(mats, scale, base=(), column=None, out_width=None, into=None):
    rows = mats[0][0].shape[0]
    width = mats[0][2][0].shape[1]
    operands = [scale]
    specs = [SMEM]
    for hi, lo, chunks in mats:
        operands += [hi, lo, *chunks]
        specs += [ANY] * (2 + len(chunks))
    operands += list(base)
    specs += [ANY] * len(base)
    aliases = {}
    if into is not None:
        aliases = {len(operands): 0}
        operands.append(into)
        specs.append(ANY)
    count = len(mats)
    sem_count = sum(2 + len(m[2]) for m in mats) + max(1, len(base))
    shape = (rows, width if column is None else out_width)
    return pl.pallas_call(
        functools.partial(apply_kernel, [len(m[2]) for m in mats], len(base), column),
        in_specs=specs,
        out_specs=VMEM if column is None else ANY,
        out_shape=jax.ShapeDtypeStruct(shape, f32),
        scratch_shapes=[
            pltpu.VMEM((count, rows, rows), bf16),
            pltpu.VMEM((count, rows, rows), bf16),
            pltpu.VMEM((count, rows, width), f32),
            pltpu.VMEM((rows, width), f32),
            pltpu.VMEM((rows, 2 * width), bf16),
            pltpu.VMEM((rows, width), f32),
            pltpu.SemaphoreType.DMA((sem_count,)),
            pltpu.SemaphoreType.DMA,
        ],
        input_output_aliases=aliases,
        compiler_params=PARAMS,
        cost_estimate=pl.CostEstimate(
            flops=count * 6 * rows * rows * width,
            bytes_accessed=count * rows * (rows * 4 + width * 4),
            transcendentals=0,
        ),
        name="apply",
    )(*operands)


def local(
    n_rows, n_bands,
    vectors, local_blocks, local_cols, coupling_blocks, coupling_cols, partners, bounds, rotation
):
    rows, band = vectors.shape
    colours, block_count, stored, size, _ = coupling_blocks.shape
    half = band // 2
    part_rows = rows // 2
    my_row = lax.axis_index("rows")
    my_band = lax.axis_index("bands")
    bits = n_rows.bit_length() - 1
    static = bits == colours
    masks = partners[:, 0]
    slots = range(colours)
    if static:
        colour_of = [
            sum(jnp.where(masks[c] == (1 << k), c, 0) for c in range(colours)).astype(jnp.int32)
            for k in slots
        ]
    else:
        colour_of = [jnp.int32(k) for k in slots]

    def to_band(x, mask):
        return lax.ppermute(x, "bands", [(i, i ^ mask) for i in range(n_bands)])

    def to_row(x, bit):
        return lax.ppermute(x, "rows", [(i, i ^ (1 << bit)) for i in range(n_rows)])

    def exchange(x, slot):
        if static:
            return to_row(x, slot)
        taken = jnp.zeros_like(x)
        for bit in range(bits):
            taken = jnp.where(masks[slot] == (1 << bit), to_row(x, bit), taken)
        return taken

    share = block_count // n_bands
    couple_parts = []
    near = [k for k in slots if static and k == 0]
    for k in slots:
        if k in near:
            count, first = block_count // 2, (my_band % 2) * (block_count // 2)
        else:
            count, first = share, my_band * share
        mine = lax.dynamic_slice(
            coupling_blocks,
            (colour_of[k], first, 0, 0, 0),
            (1, count, stored, size, size),
        )[0]
        couple_parts.append(exchange(mine, k))

    chip_mate = to_band(vectors, 1)

    others = list(range(2, n_bands, 2))

    def rotated_for(mask):
        pick = jnp.stack([my_band, my_band ^ 1, my_band ^ mask]).astype(jnp.int32)
        return rotate(vectors, chip_mate, rotation, pick, part_rows, half)

    sums = [[to_band(c, mask) for c in rotated_for(mask)] for mask in others]
    own = rotated_for(0)
    chunks = []
    for n, c in enumerate(own):
        for other in sums:
            c = c + other[n]
        chunks.append(c)
    per = rows // part_rows
    field = [chunks[h * per:(h + 1) * per] for h in range(band // half)]

    def send(parts):
        return [[exchange(c, k) for c in parts] for k in slots]

    arrived = [send(parts) for parts in field]

    far = [k for k in slots if k not in near]
    gathered = {k: [] for k in slots}
    firsts = {k: [] for k in slots}
    for k in near:
        gathered[k] = [couple_parts[k], to_band(couple_parts[k], 1)]
        firsts[k] = [(my_band % 2) * (block_count // 2), (1 - my_band % 2) * (block_count // 2)]
    joined = jnp.concatenate([couple_parts[k] for k in far], axis=0)
    for mask in range(0, n_bands, 2):
        here = joined if mask == 0 else to_band(joined, mask)
        there = to_band(here, 1)
        for which, got in ((mask, here), (mask ^ 1, there)):
            for n, k in enumerate(far):
                gathered[k].append(got[n * share:(n + 1) * share])
                firsts[k].append((my_band ^ which) * share)

    local_parts = build_local(local_blocks, local_cols, bounds)
    couple_mats = []
    for k in slots:
        if static:
            mate = my_row ^ (1 << k)
        else:
            mate = my_row ^ masks[k]
        cols = lax.dynamic_index_in_dim(coupling_cols, colour_of[k], 0, keepdims=False)
        own_cols = lax.dynamic_slice_in_dim(cols, my_row * block_count, block_count, 0)
        mate_cols = lax.dynamic_slice_in_dim(cols, mate * block_count, block_count, 0)
        meta = jnp.stack([colour_of[k], *firsts[k]]).astype(jnp.int32)
        couple_mats.append(build_couple(meta, own_cols, mate_cols, coupling_blocks, gathered[k]))

    lowest, lower, upper = (bounds[0], bounds[1], bounds[2])
    half_width = (upper - lower) / 2.0
    centre = (upper + lower) / 2.0
    sigma_one = half_width / (lowest - centre)
    sigma_two = 1.0 / (2.0 / sigma_one - sigma_one)
    scale_one = jnp.stack([sigma_one / half_width, jnp.zeros((), f32)])
    scale_two = jnp.stack([2.0 * sigma_two / half_width, -sigma_one * sigma_two])

    def terms(mine, theirs):
        return [(*local_parts, mine)] + [(*couple_mats[k], theirs[k]) for k in slots]

    first = [[apply(terms(field[h], arrived[h]), scale_one)] for h in range(2)]
    arrived = [send(parts) for parts in first]
    out = apply(terms(first[0], arrived[0]), scale_two, field[0], 0, band)
    return apply(terms(first[1], arrived[1]), scale_two, field[1], half, band, out)


def solution(mesh):
    in_specs = (
        P("rows", "bands"),
        P("rows", None, None, None),
        P("rows", None),
        P(None, "rows", None, None, None),
        P(),
        P(),
        P(),
        P(),
    )
    body = functools.partial(local, mesh.shape["rows"], mesh.shape["bands"])
    return jax.shard_map(
        body, mesh=mesh, in_specs=in_specs, out_specs=P("rows", "bands"), check_vma=False
    )
```

```python
import functools

import jax
import jax.numpy as jnp
from jax import lax
from jax.experimental import pallas as pl
from jax.experimental.pallas import tpu as pltpu
from jax.sharding import PartitionSpec as P

f32 = jnp.float32
bf16 = jnp.bfloat16
HBM = pl.BlockSpec(memory_space=pltpu.HBM)
VMEM = pl.BlockSpec(memory_space=pltpu.VMEM)
SMEM = pl.BlockSpec(memory_space=pltpu.SMEM)
PARAMS = pltpu.CompilerParams(vmem_limit_bytes=20 * 1024 * 1024)


def split(x):
    hi = x.astype(bf16)
    return hi, (x - hi.astype(f32)).astype(bf16)


def dot(a, b):
    return jnp.dot(a, b, preferred_element_type=f32)


def call(
    token, kernel, operands, specs, out_specs, out_shape, scratch, name,
    flops=0, nbytes=0, aliases=None, waits=(),
):
    ins, outs = len(operands), len(out_shape)
    first = ins + 1 + len(waits)

    def body(*refs):
        refs[first + outs][...] = jnp.zeros(token.shape, f32)
        kernel(*refs[:ins], *refs[first:first + outs], *refs[first + outs + 1:])

    *results, token = pl.pallas_call(
        body,
        in_specs=[*specs, *[pl.BlockSpec(memory_space=pl.ANY)] * (1 + len(waits))],
        out_specs=[*out_specs, VMEM],
        out_shape=[*out_shape, jax.ShapeDtypeStruct(token.shape, f32)],
        scratch_shapes=scratch,
        input_output_aliases=aliases or {},
        compiler_params=PARAMS,
        cost_estimate=pl.CostEstimate(flops=flops, bytes_accessed=nbytes, transcendentals=0),
        name=name,
    )(*operands, token, *waits)
    return results, token


def in_hbm(x):
    return pltpu.with_memory_space_constraint(x, pltpu.HBM)


def array(*shape):
    return jax.ShapeDtypeStruct(shape, f32)


def colour_of(partners_ref, slot, by_bit):
    if not by_bit:
        return jnp.int32(slot)
    colour = jnp.int32(0)
    for c in range(1, partners_ref.shape[0]):
        colour = jnp.where(partners_ref[c, 0] == (1 << slot), c, colour)
    return colour


def product(v, r):
    v_hi, v_lo = split(v)
    r_hi, r_lo = split(r)
    return dot(
        jnp.concatenate([v_hi, v_lo, v_hi], axis=1), jnp.concatenate([r_hi, r_hi, r_lo], axis=0)
    )


def band_block(index, band, width=None, part=0):
    width = width or band
    return pl.ds(pl.multiple_of(index * band + part * width, width), width)


def begin(token, vectors, rotation, partners, blocks, masks, heights, by_bit):
    rows, band = vectors.shape
    half = band // 2
    slots, tail = blocks.shape[0], blocks.shape[2:]
    wide = len(masks) * half

    def kernel(partners_ref, v_ref, rotation_ref, blocks_ref, part_ref, mate_r_ref, *refs):
        shares, (v_buf, r_buf, sems) = refs[:slots], refs[slots:]
        me = lax.axis_index("bands")
        copies = [pltpu.make_async_copy(v_ref, v_buf, sems.at[0])]
        for n, mask in enumerate(masks):
            cols = band_block(me ^ mask, band, half)
            for m, (who, dst) in enumerate(((me, r_buf), (me ^ 1, mate_r_ref))):
                src = rotation_ref.at[band_block(who, band), cols]
                dst = dst.at[:, n * half:(n + 1) * half]
                copies.append(pltpu.make_async_copy(src, dst, sems.at[1 + 2 * n + m]))
        first = len(copies)
        for slot, out in enumerate(shares):
            height = heights[slot]
            at = lax.rem(me, blocks_ref.shape[1] // height) * height
            src = blocks_ref.at[colour_of(partners_ref, slot, by_bit), pl.ds(at, height)]
            copies.append(pltpu.make_async_copy(src, out, sems.at[first + slot]))
        for c in copies:
            c.start()
        for c in copies[:first]:
            c.wait()
        part_ref[...] = product(v_buf[...], r_buf[...])
        for c in copies[first:]:
            c.wait()

    (part, mate_r, *shares), token = call(
        token, kernel,
        [in_hbm(partners), in_hbm(vectors), rotation, blocks], [SMEM, HBM, HBM, HBM],
        [VMEM] * (2 + slots),
        [array(rows, wide), array(band, wide)] + [array(n, *tail) for n in heights],
        [
            pltpu.VMEM((rows, band), f32),
            pltpu.VMEM((band, wide), f32),
            pltpu.SemaphoreType.DMA((1 + 2 * len(masks) + slots,)),
        ],
        "begin",
    )
    return part, mate_r, shares, token


def rotate_first(token, part, mate, mate_r, count):
    rows = mate.shape[0]
    half = part.shape[1] // count

    def kernel(part_ref, mate_ref, r_ref, *outs):
        total = part_ref[...] + product(mate_ref[...], r_ref[...])
        for n, out in enumerate(outs):
            out[...] = total[:, n * half:(n + 1) * half]

    return call(
        token, kernel, [part, mate, mate_r], [VMEM] * 3, [VMEM] * count,
        [array(rows, half)] * count, [], "rotate_first",
    )


def rotate_rest(token, vectors, mate, rotation, masks):
    rows, band = mate.shape
    half = band // 2
    wide = (len(masks) + 2) * half

    def kernel(v_ref, mate_ref, rotation_ref, *refs):
        others, (own_first, own_second, v_buf, r_buf, sems) = refs[:len(masks)], refs[len(masks):]
        me = lax.axis_index("bands")
        copies = [pltpu.make_async_copy(v_ref, v_buf, sems.at[0])]
        for m, who in enumerate((me, me ^ 1)):
            picks = [band_block(me ^ mask, band, half, 1) for mask in masks]
            picks += [band_block(me, band, half, h) for h in range(2)]
            for n, cols in enumerate(picks):
                src = rotation_ref.at[band_block(who, band), cols]
                dst = r_buf.at[m, :, n * half:(n + 1) * half]
                copies.append(pltpu.make_async_copy(src, dst, sems.at[1 + m * len(picks) + n]))
        for c in copies:
            c.start()
        for c in copies:
            c.wait()
        total = product(v_buf[...], r_buf[0]) + product(mate_ref[...], r_buf[1])
        for n, out in enumerate(others):
            out[...] = total[:, n * half:(n + 1) * half]
        own_first[...] = total[:, wide - 2 * half:wide - half]
        own_second[...] = total[:, wide - half:]

    out, token = call(
        token, kernel, [vectors, mate, rotation], [HBM, VMEM, HBM],
        [VMEM] * (len(masks) + 2), [array(rows, half)] * (len(masks) + 2),
        [
            pltpu.VMEM((rows, band), f32),
            pltpu.VMEM((2, band, wide), f32),
            pltpu.SemaphoreType.DMA((1 + 2 * (len(masks) + 2),)),
        ],
        "rotate_rest",
    )
    return out[:-2], out[-2], out[-1], token


def meet(token, parts, blocks=()):
    height = blocks[0].shape[0] if blocks else 0

    def kernel(*refs):
        total = refs[0][...]
        for ref in refs[1:len(parts)]:
            total = total + ref[...]
        refs[len(parts) + len(blocks)][...] = total
        for n, ref in enumerate(refs[len(parts):len(parts) + len(blocks)]):
            refs[-1][n * height:(n + 1) * height] = ref[...]

    shapes = [array(*parts[0].shape)]
    if blocks:
        shapes.append(array(len(blocks) * height, blocks[0].shape[1]))
    ins = [*parts, *blocks]
    return call(token, kernel, ins, [VMEM] * len(ins), [VMEM] * len(shapes), shapes, [], "meet")


def touch(token, waits):
    return call(token, lambda: None, [], [], [], [], [], "touch", waits=waits)[1]


def write_parts(acc, hi_ref, lo_ref):
    count, _, size, _ = acc.shape

    def one(i, carry):
        rows = pl.ds(pl.multiple_of(i * size, size), size)
        for j in range(count):
            hi, lo = split(acc[i, j])
            hi_ref[rows, j * size:(j + 1) * size] = hi
            lo_ref[rows, j * size:(j + 1) * size] = lo
        return carry

    lax.fori_loop(0, count, one, 0)


def local_kernel(cols_ref, bounds_ref, blocks_ref, hi_ref, lo_ref, acc):
    count, _, size, _ = acc.shape
    stored = blocks_ref.shape[1]
    acc[...] = jnp.zeros_like(acc)
    centre = (bounds_ref[2] + bounds_ref[1]) / 2.0
    eye = lax.broadcasted_iota(jnp.int32, (size, size), 0) == lax.broadcasted_iota(
        jnp.int32, (size, size), 1
    )
    shift = jnp.where(eye, -centre, 0.0).astype(f32)
    for i in range(count):
        acc[i, i] = shift

    def one(a, carry):
        for k in range(stored):
            block = blocks_ref[a, k]
            col = cols_ref[a * stored + k]
            acc[a, col] += block
            acc[col, a] += block.T
        return carry

    lax.fori_loop(0, count, one, 0)
    write_parts(acc, hi_ref, lo_ref)


def build_local(token, blocks, cols, bounds):
    count, stored, size, _ = blocks.shape
    rows = count * size
    return call(
        token, local_kernel, [cols, bounds, blocks], [SMEM, SMEM, VMEM],
        [VMEM, VMEM], [jax.ShapeDtypeStruct((rows, rows), bf16)] * 2,
        [pltpu.VMEM((count, count, size, size), f32)], "build_local",
    )


def build_couple(token, slot, by_bit, cols, partners, blocks, places):
    colours, count, stored, size, _ = blocks.shape
    rows = count * size
    shards = partners.shape[1]

    def kernel(cols_ref, partners_ref, blocks_ref, *refs):
        pieces, (hi_ref, lo_ref, own_buf, mate_buf, acc, sems) = refs[:len(places)], refs[len(places):]
        colour = colour_of(partners_ref, slot, by_bit)
        me = lax.axis_index("rows")
        band = lax.axis_index("bands")
        mate = me ^ (1 << slot) if by_bit else me ^ partners_ref[slot, 0]
        own_at = (colour * shards + me) * count
        mate_at = (colour * shards + mate) * count
        copies = [pltpu.make_async_copy(blocks_ref.at[colour], own_buf, sems.at[0])]
        for n, (_, start, height, _) in enumerate(places):
            long = height * stored * size
            src, dst = pieces[n].at[start:start + long], mate_buf.at[n * long:(n + 1) * long]
            copies.append(pltpu.make_async_copy(src, dst, sems.at[1 + n]))
        for c in copies:
            c.start()
        acc[...] = jnp.zeros_like(acc)
        for c in copies:
            c.wait()
        for n, (_, _, height, mask) in enumerate(places):
            first = lax.rem(band ^ mask, count // height) * height
            for i in range(height):
                a = first + i
                for k in range(stored):
                    at = ((n * height + i) * stored + k) * size
                    acc[cols_ref[(mate_at + a) * stored + k], a] += mate_buf[at:at + size].T

        def own(a, carry):
            for k in range(stored):
                acc[a, cols_ref[(own_at + a) * stored + k]] += own_buf[a, k]
            return carry

        lax.fori_loop(0, count, own, 0)
        write_parts(acc, hi_ref, lo_ref)

    return call(
        token, kernel, [cols, partners, blocks, *[in_hbm(p[0]) for p in places]],
        [SMEM, SMEM, HBM] + [HBM] * len(places),
        [VMEM, VMEM], [jax.ShapeDtypeStruct((rows, rows), bf16)] * 2,
        [
            pltpu.VMEM((count, stored, size, size), f32),
            pltpu.VMEM((count * stored * size, size), f32),
            pltpu.VMEM((count, count, size, size), f32),
            pltpu.SemaphoreType.DMA((1 + len(places),)),
        ],
        "build_couple",
    )


def scales(bounds_ref, step, shape):
    lowest, lower, upper = (jnp.full(shape, bounds_ref[i], f32) for i in range(3))
    half_width = (upper - lower) / 2.0
    centre = (upper + lower) / 2.0
    sigma_one = half_width / (lowest - centre)
    sigma_two = 1.0 / (2.0 / sigma_one - sigma_one)
    if step == 1:
        return sigma_one / half_width, None
    return 2.0 * sigma_two / half_width, -sigma_one * sigma_two


def apply_kernel(counts, step, has_partial, base_count, column, bounds_ref, *refs):
    refs = list(refs)
    mats = []
    for chunks in counts:
        hi, lo = refs.pop(0), refs.pop(0)
        mats.append((hi, lo, [refs.pop(0) for _ in range(chunks)]))
    partial = refs.pop(0) if has_partial else None
    base = [refs.pop(0) for _ in range(base_count)]
    if column is not None and column > 0:
        refs.pop(0)
    out_ref, w_buf, acc, sem = refs
    rows, width = acc.shape
    for m, (hi, lo, chunks) in enumerate(mats):
        at = 0
        for chunk in chunks:
            u_hi, u_lo = split(chunk[...])
            w_buf[at:at + chunk.shape[0], :width] = u_hi
            w_buf[at:at + chunk.shape[0], width:] = u_lo
            at += chunk.shape[0]
        both = dot(hi[...], w_buf[...])
        part = both[:, :width] + both[:, width:] + dot(lo[...], w_buf[:, :width])
        if m == 0:
            acc[...] = part
        else:
            acc[...] += part
    if step is not None:
        s_sum, s_base = scales(bounds_ref, step, (1, width))
        acc[...] = acc[...] * s_sum
    if partial is not None:
        acc[...] += partial[...]
    at = 0
    for chunk in base:
        piece = slice(at, at + chunk.shape[0])
        acc[piece] += chunk[...] * s_base
        at += chunk.shape[0]
    if column is None:
        out_ref[...] = acc[...]
    else:
        c = pltpu.make_async_copy(acc, out_ref.at[:, column:column + width], sem)
        c.start()
        c.wait()


def apply(
    token, bounds, mats, step=None, partial=None, base=(), column=None, out_width=None, into=None,
    late=False, waits=()):
    rows = mats[0][0].shape[0]
    width = mats[0][2][0].shape[1]
    operands = [bounds]
    specs = [SMEM]
    for hi, lo, chunks in mats:
        operands += [hi, lo, *chunks]
        specs += [VMEM] * (2 + len(chunks))
    if partial is not None:
        operands.append(partial)
        specs.append(VMEM)
    operands += list(base)
    specs += [VMEM] * len(base)
    aliases = {}
    if into is not None:
        aliases = {len(operands): 0}
        operands.append(into)
        specs.append(HBM)
    shape = array(rows, width if column is None else out_width)
    kernel = functools.partial(
        apply_kernel, [len(m[2]) for m in mats], step, partial is not None, len(base), column
    )
    (out,), token = call(
        token, kernel, operands, specs, [VMEM if column is None else HBM], [shape],
        [
            pltpu.VMEM((rows, 2 * width), bf16),
            pltpu.VMEM((rows, width), f32),
            pltpu.SemaphoreType.DMA,
        ],
        "apply",
        len(mats) * 6 * rows * rows * width if late else 0,
        len(mats) * rows * rows * 4 if late else 0,
        aliases,
        waits,
    )
    return out, token


def gate(x, *after):
    return lax.optimization_barrier((x, *after))[0]


def local(
    n_rows, n_bands,
    vectors, local_blocks, local_cols, coupling_blocks, coupling_cols, partners, bounds, rotation
):
    rows, band = vectors.shape
    colours, block_count = coupling_blocks.shape[:2]
    half = band // 2
    bits = n_rows.bit_length() - 1
    by_bit = bits == colours
    slots = range(colours)

    def to_band(x, mask):
        return lax.ppermute(x, "bands", [(i, i ^ mask) for i in range(n_bands)])

    def to_row(x, bit):
        return lax.ppermute(x, "rows", [(i, i ^ (1 << bit)) for i in range(n_rows)])

    def exchange(x, slot):
        if by_bit:
            return to_row(x, slot)
        taken = jnp.zeros_like(x)
        for bit in range(bits):
            taken = jnp.where(partners[slot, 0] == (1 << bit), to_row(x, bit), taken)
        return taken

    blocks = in_hbm(coupling_blocks)
    spin = in_hbm(rotation)
    flat_cols = coupling_cols.reshape(-1)
    token = jnp.zeros((8, 128), f32)

    chip_mate = to_band(vectors, 1)

    masks = list(range(2, n_bands, 2))
    order = list(slots)[::-1]
    near = [k for k in slots if by_bit and k == 0]
    far = [k for k in slots if k not in near]
    heights = [block_count // (2 if k in near else n_bands) for k in slots]
    stored = coupling_blocks.shape[2]
    vecs = in_hbm(vectors)
    part, mate_r, shares, token = begin(token, vecs, spin, partners, blocks, masks, heights, by_bit)
    sent, token = rotate_first(token, part, chip_mate, mate_r, len(masks))
    came = [to_band(c, mask) for c, mask in zip(sent, masks)]
    second, own_first, own_second, token = rotate_rest(token, vecs, chip_mate, spin, masks)
    shares = [s.reshape(-1, s.shape[-1]) for s in shares]
    shares = {k: exchange(gate(shares[k], token) if k in near else shares[k], k) for k in order}
    (total, joined), token = meet(token, [own_first, *came], [shares[k] for k in far])
    later = [to_band(gate(c, token), mask) for c, mask in zip(second, masks)]
    field = [total]
    held = {0: joined, 1: to_band(joined, 1)}
    passed = [to_band(joined, mask) for mask in masks]

    def send(part, after=None):
        return {k: exchange(gate(part, after) if k in near and after is not None else part, k) for k in order}

    def part_sum(terms, *rest, **options):
        nonlocal token
        out, token = apply(token, bounds, terms, *rest, **options)
        return out

    arrived = [send(total)]
    (total,), token = meet(token, [own_second, *later])
    field.append(total)
    local_parts, token = build_local(token, local_blocks, local_cols.reshape(-1), bounds)
    waits = [shares[k] for k in near] + [held[1]]
    partial = [part_sum([(*local_parts, [field[0]])], 1, waits=waits)]
    partial.append(part_sum([(*local_parts, [field[1]])], 1))
    token = touch(token, [arrived[0][k] for k in slots])

    for mask, x in zip(masks, passed):
        held[mask] = gate(x, token)
        held[mask ^ 1] = to_band(held[mask], 1)
    for k in near:
        shares[k] = gate(shares[k], token)
    total = gate(total, token)
    size = coupling_blocks.shape[-1]
    mats = {}
    for k in far + near:
        if k in near:
            places = [(shares[k], 0, heights[k], 0), (to_band(shares[k], 1), 0, heights[k], 1)]
        else:
            at = far.index(k) * heights[k] * stored * size
            places = [(x, at, heights[k], m) for m, x in held.items()]
        mats[k], token = build_couple(token, k, by_bit, flat_cols, partners, blocks, places)
        if k == far[0]:
            arrived.append(send(total, token))
    first = []
    for h in range(2):
        terms = [(*mats[k], [arrived[h][k]]) for k in slots]
        first.append(part_sum(terms, 1, partial[h]))
    arrived = [send(f) for f in first]
    out = None
    for h in range(2):
        terms = [(*local_parts, [first[h]])] + [(*mats[k], [arrived[h][k]]) for k in near]
        early = part_sum(terms, 2, None, [field[h]], late=True)
        for k in far[:-1]:
            early = part_sum([(*mats[k], [arrived[h][k]])], 2, early, late=True)
        k = far[-1]
        out = part_sum([(*mats[k], [arrived[h][k]])], 2, early, (), h * half, band, out, late=True)
    return out


def solution(mesh):
    in_specs = (
        P("rows", "bands"),
        P("rows", None, None, None),
        P("rows", None),
        P(None, "rows", None, None, None),
        P(),
        P(),
        P(),
        P(),
    )
    body = functools.partial(local, mesh.shape["rows"], mesh.shape["bands"])
    return jax.shard_map(
        body, mesh=mesh, in_specs=in_specs, out_specs=P("rows", "bands"), check_vma=False
    )
```

```python
import functools

import jax
import jax.numpy as jnp
from jax import lax
from jax.experimental import pallas as pl
from jax.experimental.pallas import tpu as pltpu
from jax.sharding import PartitionSpec as P

f32 = jnp.float32
bf16 = jnp.bfloat16
HBM = pl.BlockSpec(memory_space=pltpu.HBM)
VMEM = pl.BlockSpec(memory_space=pltpu.VMEM)
SMEM = pl.BlockSpec(memory_space=pltpu.SMEM)
PARAMS = pltpu.CompilerParams(vmem_limit_bytes=20 * 1024 * 1024)


def split(x):
    hi = x.astype(bf16)
    return hi, (x - hi.astype(f32)).astype(bf16)


def dot(a, b):
    return jnp.dot(a, b, preferred_element_type=f32)


def call(
    token, kernel, operands, specs, out_specs, out_shape, scratch, name,
    aliases=None, waits=(), last=False,
):
    ins, outs = len(operands), len(out_shape)
    first = ins + 1 + len(waits)
    given = [] if last else [jax.ShapeDtypeStruct(token.shape, f32)]

    def body(*refs):
        for ref in refs[first + outs:first + outs + len(given)]:
            ref[...] = jnp.zeros(token.shape, f32)
        kernel(*refs[:ins], *refs[first:first + outs], *refs[first + outs + len(given):])

    results = pl.pallas_call(
        body,
        in_specs=[*specs, *[pl.BlockSpec(memory_space=pl.ANY)] * (1 + len(waits))],
        out_specs=[*out_specs, *[VMEM] * len(given)],
        out_shape=[*out_shape, *given],
        scratch_shapes=scratch,
        input_output_aliases=aliases or {},
        compiler_params=PARAMS,
        cost_estimate=pl.CostEstimate(flops=0, bytes_accessed=0, transcendentals=0),
        name=name,
    )(*operands, token, *waits)
    return results[:outs], (None if last else results[outs])


def in_hbm(x):
    return pltpu.with_memory_space_constraint(x, pltpu.HBM)


def array(*shape):
    return jax.ShapeDtypeStruct(shape, f32)


def colour_of(partners_ref, slot, by_bit):
    if not by_bit:
        return jnp.int32(slot)
    colour = jnp.int32(0)
    for c in range(1, partners_ref.shape[0]):
        colour = jnp.where(partners_ref[c, 0] == (1 << slot), c, colour)
    return colour


def product(v, r):
    v_hi, v_lo = split(v)
    r_hi, r_lo = split(r)
    return dot(
        jnp.concatenate([v_hi, v_lo, v_hi], axis=1), jnp.concatenate([r_hi, r_hi, r_lo], axis=0)
    )


def band_block(index, band, width=None, part=0):
    width = width or band
    return pl.ds(pl.multiple_of(index * band + part * width, width), width)


def begin(token, vectors, rotation, partners, blocks, masks, heights, by_bit):
    rows, band = vectors.shape
    half = band // 2
    slots, tail = blocks.shape[0], blocks.shape[2:]
    wide = len(masks) * half

    def kernel(partners_ref, v_ref, rotation_ref, blocks_ref, part_ref, mate_r_ref, *refs):
        shares, (v_buf, r_buf, sems) = refs[:slots], refs[slots:]
        me = lax.axis_index("bands")
        copies = [pltpu.make_async_copy(v_ref, v_buf, sems.at[0])]
        for n, mask in enumerate(masks):
            cols = band_block(me ^ mask, band, half)
            for m, (who, dst) in enumerate(((me, r_buf), (me ^ 1, mate_r_ref))):
                src = rotation_ref.at[band_block(who, band), cols]
                dst = dst.at[:, n * half:(n + 1) * half]
                copies.append(pltpu.make_async_copy(src, dst, sems.at[1 + 2 * n + m]))
        first = len(copies)
        for slot, out in enumerate(shares):
            height = heights[slot]
            at = lax.rem(me, blocks_ref.shape[1] // height) * height
            src = blocks_ref.at[colour_of(partners_ref, slot, by_bit), pl.ds(at, height)]
            copies.append(pltpu.make_async_copy(src, out, sems.at[first + slot]))
        for c in copies:
            c.start()
        for c in copies[:first]:
            c.wait()
        part_ref[...] = product(v_buf[...], r_buf[...])
        for c in copies[first:]:
            c.wait()

    (part, mate_r, *shares), token = call(
        token, kernel,
        [in_hbm(partners), in_hbm(vectors), rotation, blocks], [SMEM, HBM, HBM, HBM],
        [VMEM] * (2 + slots),
        [array(rows, wide), array(band, wide)] + [array(n, *tail) for n in heights],
        [
            pltpu.VMEM((rows, band), f32),
            pltpu.VMEM((band, wide), f32),
            pltpu.SemaphoreType.DMA((1 + 2 * len(masks) + slots,)),
        ],
        "begin",
    )
    return part, mate_r, shares, token


def rotate_first(token, part, mate, mate_r, count):
    rows = mate.shape[0]
    half = part.shape[1] // count

    def kernel(part_ref, mate_ref, r_ref, *outs):
        total = part_ref[...] + product(mate_ref[...], r_ref[...])
        for n, out in enumerate(outs):
            out[...] = total[:, n * half:(n + 1) * half]

    return call(
        token, kernel, [part, mate, mate_r], [VMEM] * 3, [VMEM] * count,
        [array(rows, half)] * count, [], "rotate_first",
    )


def rotate_rest(token, vectors, mate, rotation, masks):
    rows, band = mate.shape
    half = band // 2
    wide = (len(masks) + 2) * half

    def kernel(v_ref, mate_ref, rotation_ref, *refs):
        others, (own_first, own_second, v_buf, r_buf, sems) = refs[:len(masks)], refs[len(masks):]
        me = lax.axis_index("bands")
        copies = [pltpu.make_async_copy(v_ref, v_buf, sems.at[0])]
        for m, who in enumerate((me, me ^ 1)):
            picks = [band_block(me ^ mask, band, half, 1) for mask in masks]
            picks += [band_block(me, band, half, h) for h in range(2)]
            for n, cols in enumerate(picks):
                src = rotation_ref.at[band_block(who, band), cols]
                dst = r_buf.at[m, :, n * half:(n + 1) * half]
                copies.append(pltpu.make_async_copy(src, dst, sems.at[1 + m * len(picks) + n]))
        for c in copies:
            c.start()
        for c in copies:
            c.wait()
        total = product(v_buf[...], r_buf[0]) + product(mate_ref[...], r_buf[1])
        for n, out in enumerate(others):
            out[...] = total[:, n * half:(n + 1) * half]
        own_first[...] = total[:, wide - 2 * half:wide - half]
        own_second[...] = total[:, wide - half:]

    out, token = call(
        token, kernel, [vectors, mate, rotation], [HBM, VMEM, HBM],
        [VMEM] * (len(masks) + 2), [array(rows, half)] * (len(masks) + 2),
        [
            pltpu.VMEM((rows, band), f32),
            pltpu.VMEM((2, band, wide), f32),
            pltpu.SemaphoreType.DMA((1 + 2 * (len(masks) + 2),)),
        ],
        "rotate_rest",
    )
    return out[:-2], out[-2], out[-1], token


def meet(token, parts, blocks=(), waits=()):
    height = blocks[0].shape[0] if blocks else 0

    def kernel(*refs):
        total = refs[0][...]
        for ref in refs[1:len(parts)]:
            total = total + ref[...]
        refs[len(parts) + len(blocks)][...] = total
        for n, ref in enumerate(refs[len(parts):len(parts) + len(blocks)]):
            refs[-1][n * height:(n + 1) * height] = ref[...]

    shapes = [array(*parts[0].shape)]
    if blocks:
        shapes.append(array(len(blocks) * height, blocks[0].shape[1]))
    ins = [*parts, *blocks]
    return call(token, kernel, ins, [VMEM] * len(ins), [VMEM] * len(shapes), shapes, [], "meet", waits=waits)


def touch(token, waits):
    return call(token, lambda: None, [], [], [], [], [], "touch", waits=waits)[1]


def write_parts(acc, hi_ref, lo_ref):
    count, _, size, _ = acc.shape

    def one(i, carry):
        rows = pl.ds(pl.multiple_of(i * size, size), size)
        for j in range(count):
            hi, lo = split(acc[i, j])
            hi_ref[rows, j * size:(j + 1) * size] = hi
            lo_ref[rows, j * size:(j + 1) * size] = lo
        return carry

    lax.fori_loop(0, count, one, 0)


def local_kernel(cols_ref, bounds_ref, blocks_ref, hi_ref, lo_ref, acc):
    count, _, size, _ = acc.shape
    stored = blocks_ref.shape[1]
    acc[...] = jnp.zeros_like(acc)
    centre = (bounds_ref[2] + bounds_ref[1]) / 2.0
    eye = lax.broadcasted_iota(jnp.int32, (size, size), 0) == lax.broadcasted_iota(
        jnp.int32, (size, size), 1
    )
    shift = jnp.where(eye, -centre, 0.0).astype(f32)
    for i in range(count):
        acc[i, i] = shift

    def one(a, carry):
        for k in range(stored):
            block = blocks_ref[a, k]
            col = cols_ref[a * stored + k]
            acc[a, col] += block
            acc[col, a] += block.T
        return carry

    lax.fori_loop(0, count, one, 0)
    write_parts(acc, hi_ref, lo_ref)


def build_local(token, blocks, cols, bounds):
    count, stored, size, _ = blocks.shape
    rows = count * size
    return call(
        token, local_kernel, [cols, bounds, blocks], [SMEM, SMEM, VMEM],
        [VMEM, VMEM], [jax.ShapeDtypeStruct((rows, rows), bf16)] * 2,
        [pltpu.VMEM((count, count, size, size), f32)], "build_local",
    )


def build_couple(token, slot, by_bit, cols, partners, blocks, places):
    colours, count, stored, size, _ = blocks.shape
    rows = count * size
    shards = partners.shape[1]

    def kernel(cols_ref, partners_ref, blocks_ref, *refs):
        pieces, (hi_ref, lo_ref, own_buf, mate_buf, acc, sems) = refs[:len(places)], refs[len(places):]
        colour = colour_of(partners_ref, slot, by_bit)
        me = lax.axis_index("rows")
        band = lax.axis_index("bands")
        mate = me ^ (1 << slot) if by_bit else me ^ partners_ref[slot, 0]
        own_at = (colour * shards + me) * count
        mate_at = (colour * shards + mate) * count
        copies = [pltpu.make_async_copy(blocks_ref.at[colour], own_buf, sems.at[0])]
        for n, (_, start, height, _) in enumerate(places):
            long = height * stored * size
            src, dst = pieces[n].at[start:start + long], mate_buf.at[n * long:(n + 1) * long]
            copies.append(pltpu.make_async_copy(src, dst, sems.at[1 + n]))
        for c in copies:
            c.start()
        acc[...] = jnp.zeros_like(acc)
        for c in copies:
            c.wait()
        for n, (_, _, height, mask) in enumerate(places):
            first = lax.rem(band ^ mask, count // height) * height
            for i in range(height):
                a = first + i
                for k in range(stored):
                    at = ((n * height + i) * stored + k) * size
                    acc[cols_ref[(mate_at + a) * stored + k], a] += mate_buf[at:at + size].T

        def own(a, carry):
            for k in range(stored):
                acc[a, cols_ref[(own_at + a) * stored + k]] += own_buf[a, k]
            return carry

        lax.fori_loop(0, count, own, 0)
        write_parts(acc, hi_ref, lo_ref)

    return call(
        token, kernel, [cols, partners, blocks, *[in_hbm(p[0]) for p in places]],
        [SMEM, SMEM, HBM] + [HBM] * len(places),
        [VMEM, VMEM], [jax.ShapeDtypeStruct((rows, rows), bf16)] * 2,
        [
            pltpu.VMEM((count, stored, size, size), f32),
            pltpu.VMEM((count * stored * size, size), f32),
            pltpu.VMEM((count, count, size, size), f32),
            pltpu.SemaphoreType.DMA((1 + len(places),)),
        ],
        "build_couple",
    )


def scales(bounds_ref, step, shape):
    lowest, lower, upper = (jnp.full(shape, bounds_ref[i], f32) for i in range(3))
    half_width = (upper - lower) / 2.0
    centre = (upper + lower) / 2.0
    sigma_one = half_width / (lowest - centre)
    sigma_two = 1.0 / (2.0 / sigma_one - sigma_one)
    if step == 1:
        return sigma_one / half_width, None
    return 2.0 * sigma_two / half_width, -sigma_one * sigma_two


def apply_kernel(counts, step, has_partial, base_count, column, bounds_ref, *refs):
    refs = list(refs)
    mats = []
    for chunks in counts:
        hi, lo = refs.pop(0), refs.pop(0)
        mats.append((hi, lo, [refs.pop(0) for _ in range(chunks)]))
    partial = refs.pop(0) if has_partial else None
    base = [refs.pop(0) for _ in range(base_count)]
    if column is not None and column > 0:
        refs.pop(0)
    out_ref, w_buf, acc, sems = refs
    rows, width = acc.shape
    tiles = 1 if column is None else 4
    height = rows // tiles
    if step is not None:
        s_sum, s_base = scales(bounds_ref, step, (1, width))
    for m, (_, _, chunks) in enumerate(mats):
        at = 0
        for chunk in chunks:
            u_hi, u_lo = split(chunk[...])
            w_buf[m, at:at + chunk.shape[0], :width] = u_hi
            w_buf[m, at:at + chunk.shape[0], width:] = u_lo
            at += chunk.shape[0]
    copies = []
    for t in range(tiles):
        tile = slice(t * height, (t + 1) * height)
        for m, (hi, lo, _) in enumerate(mats):
            both = dot(hi[tile], w_buf[m])
            part = both[:, :width] + both[:, width:] + dot(lo[tile], w_buf[m, :, :width])
            if m == 0:
                acc[tile] = part
            else:
                acc[tile] += part
        result = acc[tile]
        if step is not None:
            result = result * s_sum
        if partial is not None:
            result = result + partial[tile]
        for chunk in base:
            result = result + chunk[tile] * s_base
        if column is None:
            out_ref[tile] = result
        else:
            acc[tile] = result
            dst = out_ref.at[tile, column:column + width]
            copies.append(pltpu.make_async_copy(acc.at[tile], dst, sems.at[t]))
            copies[-1].start()
    for c in copies:
        c.wait()


def apply(
    token, bounds, mats, step=None, partial=None, base=(), column=None, out_width=None, into=None,
    waits=(), last=False,
):
    rows = mats[0][0].shape[0]
    width = mats[0][2][0].shape[1]
    operands = [bounds]
    specs = [SMEM]
    for hi, lo, chunks in mats:
        operands += [hi, lo, *chunks]
        specs += [VMEM] * (2 + len(chunks))
    if partial is not None:
        operands.append(partial)
        specs.append(VMEM)
    operands += list(base)
    specs += [VMEM] * len(base)
    aliases = {}
    if into is not None:
        aliases = {len(operands): 0}
        operands.append(into)
        specs.append(HBM)
    shape = array(rows, width if column is None else out_width)
    kernel = functools.partial(
        apply_kernel, [len(m[2]) for m in mats], step, partial is not None, len(base), column
    )
    (out,), token = call(
        token, kernel, operands, specs, [VMEM if column is None else HBM], [shape],
        [
            pltpu.VMEM((len(mats), rows, 2 * width), bf16),
            pltpu.VMEM((rows, width), f32),
            pltpu.SemaphoreType.DMA((8,)),
        ],
        "apply", aliases, waits, last,
    )
    return out, token


def gate(x, *after):
    return lax.optimization_barrier((x, *after))[0]


def local(
    n_rows, n_bands,
    vectors, local_blocks, local_cols, coupling_blocks, coupling_cols, partners, bounds, rotation
):
    rows, band = vectors.shape
    colours, block_count = coupling_blocks.shape[:2]
    half = band // 2
    bits = n_rows.bit_length() - 1
    by_bit = bits == colours
    slots = range(colours)

    def to_band(x, mask):
        return lax.ppermute(x, "bands", [(i, i ^ mask) for i in range(n_bands)])

    def to_row(x, bit):
        return lax.ppermute(x, "rows", [(i, i ^ (1 << bit)) for i in range(n_rows)])

    def exchange(x, slot):
        if by_bit:
            return to_row(x, slot)
        taken = jnp.zeros_like(x)
        for bit in range(bits):
            taken = jnp.where(partners[slot, 0] == (1 << bit), to_row(x, bit), taken)
        return taken

    blocks = in_hbm(coupling_blocks)
    spin = in_hbm(rotation)
    flat_cols = coupling_cols.reshape(-1)
    token = jnp.zeros((8, 128), f32)

    chip_mate = to_band(vectors, 1)

    masks = list(range(2, n_bands, 2))
    order = list(slots)[::-1]
    near = [k for k in slots if by_bit and k == 0]
    far = [k for k in slots if k not in near]
    heights = [block_count // (2 if k in near else n_bands) for k in slots]
    stored = coupling_blocks.shape[2]
    vecs = in_hbm(vectors)
    part, mate_r, shares, token = begin(token, vecs, spin, partners, blocks, masks, heights, by_bit)
    sent, token = rotate_first(token, part, chip_mate, mate_r, len(masks))
    came = [to_band(c, mask) for c, mask in zip(sent, masks)]
    second, own_first, own_second, token = rotate_rest(token, vecs, chip_mate, spin, masks)
    shares = [s.reshape(-1, s.shape[-1]) for s in shares]
    shares = {k: exchange(gate(shares[k], token) if k in near else shares[k], k) for k in order}
    (total, joined), token = meet(token, [own_first, *came], [shares[k] for k in far])
    later = [to_band(gate(c, token), mask) for c, mask in zip(second, masks)]
    field = [total]
    passed = [to_band(joined, mask) for mask in masks]

    def send(part, after=None):
        return {k: exchange(gate(part, after) if k in near and after is not None else part, k) for k in order}

    def part_sum(terms, *rest, **options):
        nonlocal token
        out, token = apply(token, bounds, terms, *rest, **options)
        return out

    (total,), token = meet(token, [own_second, *later], (), [shares[k] for k in near])
    field.append(total)
    arrived = [send(field[0], token)]
    local_parts, token = build_local(token, local_blocks, local_cols.reshape(-1), bounds)
    waits = []
    partial = [part_sum([(*local_parts, [field[0]])], 1, waits=waits)]
    partial.append(part_sum([(*local_parts, [field[1]])], 1))
    token = touch(token, [arrived[0][k] for k in slots])

    total = gate(total, token)
    arrived.append({k: exchange(total, k) for k in far})

    held = {}
    for mask, x in zip([0, *masks], [joined, *passed]):
        held[mask] = gate(x, token)
        held[mask ^ 1] = to_band(held[mask], 1)
    for k in near:
        shares[k] = gate(shares[k], token)
    size = coupling_blocks.shape[-1]
    mats = {}
    for k in far + near:
        if k in near:
            places = [(shares[k], 0, heights[k], 0), (to_band(shares[k], 1), 0, heights[k], 1)]
        else:
            at = far.index(k) * heights[k] * stored * size
            places = [(x, at, heights[k], m) for m, x in held.items()]
        mats[k], token = build_couple(token, k, by_bit, flat_cols, partners, blocks, places)
        if k == far[0] and near:
            arrived[1].update({n: exchange(gate(total, token), n) for n in near})
    first = []
    for h in range(2):
        terms = [(*mats[k], [arrived[h][k]]) for k in slots]
        first.append(part_sum(terms, 1, partial[h]))
    arrived = [send(f) for f in first]
    out = None
    for h in range(2):
        terms = [(*local_parts, [first[h]])] + [(*mats[k], [arrived[h][k]]) for k in near]
        early = part_sum(terms, 2, None, [field[h]])
        for k in far[:-1]:
            early = part_sum([(*mats[k], [arrived[h][k]])], 2, early)
        k = far[-1]
        out = part_sum([(*mats[k], [arrived[h][k]])], 2, early, (), h * half, band, out, last=h == 1)
    return out


def solution(mesh):
    in_specs = (
        P("rows", "bands"),
        P("rows", None, None, None),
        P("rows", None),
        P(None, "rows", None, None, None),
        P(),
        P(),
        P(),
        P(),
    )
    body = functools.partial(local, mesh.shape["rows"], mesh.shape["bands"])
    return jax.shard_map(
        body, mesh=mesh, in_specs=in_specs, out_specs=P("rows", "bands"), check_vma=False
    )
```

```python
import functools

import jax
import jax.numpy as jnp
from jax import lax
from jax.experimental import pallas as pl
from jax.experimental.pallas import tpu as pltpu
from jax.sharding import PartitionSpec as P

f32 = jnp.float32
bf16 = jnp.bfloat16
HBM = pl.BlockSpec(memory_space=pltpu.HBM)
VMEM = pl.BlockSpec(memory_space=pltpu.VMEM)
SMEM = pl.BlockSpec(memory_space=pltpu.SMEM)
PARAMS = pltpu.CompilerParams(vmem_limit_bytes=20 * 1024 * 1024)


def split(x):
    hi = x.astype(bf16)
    return hi, (x - hi.astype(f32)).astype(bf16)


def dot(a, b):
    return jnp.dot(a, b, preferred_element_type=f32)


def call(
    token, kernel, operands, specs, out_specs, out_shape, scratch, name,
    aliases=None, waits=(), last=False,
):
    ins, outs = len(operands), len(out_shape)
    first = ins + 1 + len(waits)
    given = [] if last else [jax.ShapeDtypeStruct(token.shape, f32)]

    def body(*refs):
        for ref in refs[first + outs:first + outs + len(given)]:
            ref[...] = jnp.zeros(token.shape, f32)
        kernel(*refs[:ins], *refs[first:first + outs], *refs[first + outs + len(given):])

    results = pl.pallas_call(
        body,
        in_specs=[*specs, *[pl.BlockSpec(memory_space=pl.ANY)] * (1 + len(waits))],
        out_specs=[*out_specs, *[VMEM] * len(given)],
        out_shape=[*out_shape, *given],
        scratch_shapes=scratch,
        input_output_aliases=aliases or {},
        compiler_params=PARAMS,
        cost_estimate=pl.CostEstimate(flops=0, bytes_accessed=0, transcendentals=0),
        name=name,
    )(*operands, token, *waits)
    return results[:outs], (None if last else results[outs])


def in_hbm(x):
    return pltpu.with_memory_space_constraint(x, pltpu.HBM)


def array(*shape):
    return jax.ShapeDtypeStruct(shape, f32)


def colour_of(partners_ref, slot, by_bit):
    if not by_bit:
        return jnp.int32(slot)
    colour = jnp.int32(0)
    for c in range(1, partners_ref.shape[0]):
        colour = jnp.where(partners_ref[c, 0] == (1 << slot), c, colour)
    return colour


def product(v, r):
    v_hi, v_lo = split(v)
    r_hi, r_lo = split(r)
    return dot(
        jnp.concatenate([v_hi, v_lo, v_hi], axis=1), jnp.concatenate([r_hi, r_hi, r_lo], axis=0)
    )


def band_block(index, band, width=None, part=0):
    width = width or band
    return pl.ds(pl.multiple_of(index * band + part * width, width), width)


def begin(token, vectors, rotation, partners, blocks, masks, heights, by_bit):
    rows, band = vectors.shape
    half = band // 2
    slots, tail = blocks.shape[0], blocks.shape[2:]
    wide = len(masks) * half

    def kernel(partners_ref, v_ref, rotation_ref, blocks_ref, part_ref, mate_r_ref, *refs):
        shares, (v_buf, r_buf, sems) = refs[:slots], refs[slots:]
        me = lax.axis_index("bands")
        copies = [pltpu.make_async_copy(v_ref, v_buf, sems.at[0])]
        for n, mask in enumerate(masks):
            cols = band_block(me ^ mask, band, half)
            for m, (who, dst) in enumerate(((me, r_buf), (me ^ 1, mate_r_ref))):
                src = rotation_ref.at[band_block(who, band), cols]
                dst = dst.at[:, n * half:(n + 1) * half]
                copies.append(pltpu.make_async_copy(src, dst, sems.at[1 + 2 * n + m]))
        first = len(copies)
        for slot, out in enumerate(shares):
            height = heights[slot]
            at = lax.rem(me, blocks_ref.shape[1] // height) * height
            src = blocks_ref.at[colour_of(partners_ref, slot, by_bit), pl.ds(at, height)]
            copies.append(pltpu.make_async_copy(src, out, sems.at[first + slot]))
        for c in copies:
            c.start()
        for c in copies[:first]:
            c.wait()
        part_ref[...] = product(v_buf[...], r_buf[...])
        for c in copies[first:]:
            c.wait()

    (part, mate_r, *shares), token = call(
        token, kernel,
        [in_hbm(partners), in_hbm(vectors), rotation, blocks], [SMEM, HBM, HBM, HBM],
        [VMEM] * (2 + slots),
        [array(rows, wide), array(band, wide)] + [array(n, *tail) for n in heights],
        [
            pltpu.VMEM((rows, band), f32),
            pltpu.VMEM((band, wide), f32),
            pltpu.SemaphoreType.DMA((1 + 2 * len(masks) + slots,)),
        ],
        "begin",
    )
    return part, mate_r, shares, token


def rotate_first(token, part, mate, mate_r, count):
    rows = mate.shape[0]
    half = part.shape[1] // count

    def kernel(part_ref, mate_ref, r_ref, *outs):
        total = part_ref[...] + product(mate_ref[...], r_ref[...])
        for n, out in enumerate(outs):
            out[...] = total[:, n * half:(n + 1) * half]

    return call(
        token, kernel, [part, mate, mate_r], [VMEM] * 3, [VMEM] * count,
        [array(rows, half)] * count, [], "rotate_first",
    )


def rotate_rest(token, vectors, mate, rotation, masks):
    rows, band = mate.shape
    half = band // 2
    wide = (len(masks) + 2) * half

    def kernel(v_ref, mate_ref, rotation_ref, *refs):
        others, (own_first, own_second, v_buf, r_buf, sems) = refs[:len(masks)], refs[len(masks):]
        me = lax.axis_index("bands")
        copies = [pltpu.make_async_copy(v_ref, v_buf, sems.at[0])]
        for m, who in enumerate((me, me ^ 1)):
            picks = [band_block(me ^ mask, band, half, 1) for mask in masks]
            picks += [band_block(me, band, half, h) for h in range(2)]
            for n, cols in enumerate(picks):
                src = rotation_ref.at[band_block(who, band), cols]
                dst = r_buf.at[m, :, n * half:(n + 1) * half]
                copies.append(pltpu.make_async_copy(src, dst, sems.at[1 + m * len(picks) + n]))
        for c in copies:
            c.start()
        for c in copies:
            c.wait()
        total = product(v_buf[...], r_buf[0]) + product(mate_ref[...], r_buf[1])
        for n, out in enumerate(others):
            out[...] = total[:, n * half:(n + 1) * half]
        own_first[...] = total[:, wide - 2 * half:wide - half]
        own_second[...] = total[:, wide - half:]

    out, token = call(
        token, kernel, [vectors, mate, rotation], [HBM, VMEM, HBM],
        [VMEM] * (len(masks) + 2), [array(rows, half)] * (len(masks) + 2),
        [
            pltpu.VMEM((rows, band), f32),
            pltpu.VMEM((2, band, wide), f32),
            pltpu.SemaphoreType.DMA((1 + 2 * (len(masks) + 2),)),
        ],
        "rotate_rest",
    )
    return out[:-2], out[-2], out[-1], token


def meet(token, parts, blocks=(), waits=()):
    height = blocks[0].shape[0] if blocks else 0

    def kernel(*refs):
        total = refs[0][...]
        for ref in refs[1:len(parts)]:
            total = total + ref[...]
        refs[len(parts) + len(blocks)][...] = total
        for n, ref in enumerate(refs[len(parts):len(parts) + len(blocks)]):
            refs[-1][n * height:(n + 1) * height] = ref[...]

    shapes = [array(*parts[0].shape)]
    if blocks:
        shapes.append(array(len(blocks) * height, blocks[0].shape[1]))
    ins = [*parts, *blocks]
    return call(token, kernel, ins, [VMEM] * len(ins), [VMEM] * len(shapes), shapes, [], "meet", waits=waits)


def touch(token, waits):
    return call(token, lambda: None, [], [], [], [], [], "touch", waits=waits)[1]


def write_parts(acc, hi_ref, lo_ref):
    count, _, size, _ = acc.shape

    def one(i, carry):
        rows = pl.ds(pl.multiple_of(i * size, size), size)
        for j in range(count):
            hi, lo = split(acc[i, j])
            hi_ref[rows, j * size:(j + 1) * size] = hi
            lo_ref[rows, j * size:(j + 1) * size] = lo
        return carry

    lax.fori_loop(0, count, one, 0)


def local_kernel(cols_ref, bounds_ref, blocks_ref, hi_ref, lo_ref, acc):
    count, _, size, _ = acc.shape
    stored = blocks_ref.shape[1]
    acc[...] = jnp.zeros_like(acc)
    centre = (bounds_ref[2] + bounds_ref[1]) / 2.0
    eye = lax.broadcasted_iota(jnp.int32, (size, size), 0) == lax.broadcasted_iota(
        jnp.int32, (size, size), 1
    )
    shift = jnp.where(eye, -centre, 0.0).astype(f32)
    for i in range(count):
        acc[i, i] = shift

    def one(a, carry):
        for k in range(stored):
            block = blocks_ref[a, k]
            col = cols_ref[a * stored + k]
            acc[a, col] += block
            acc[col, a] += block.T
        return carry

    lax.fori_loop(0, count, one, 0)
    write_parts(acc, hi_ref, lo_ref)


def build_local(token, blocks, cols, bounds):
    count, stored, size, _ = blocks.shape
    rows = count * size
    return call(
        token, local_kernel, [cols, bounds, blocks], [SMEM, SMEM, VMEM],
        [VMEM, VMEM], [jax.ShapeDtypeStruct((rows, rows), bf16)] * 2,
        [pltpu.VMEM((count, count, size, size), f32)], "build_local",
    )


def build_couple(token, slot, by_bit, cols, partners, blocks, places):
    colours, count, stored, size, _ = blocks.shape
    rows = count * size
    shards = partners.shape[1]

    def kernel(cols_ref, partners_ref, blocks_ref, *refs):
        pieces, (hi_ref, lo_ref, own_buf, mate_buf, acc, sems) = refs[:len(places)], refs[len(places):]
        colour = colour_of(partners_ref, slot, by_bit)
        me = lax.axis_index("rows")
        band = lax.axis_index("bands")
        mate = me ^ (1 << slot) if by_bit else me ^ partners_ref[slot, 0]
        own_at = (colour * shards + me) * count
        mate_at = (colour * shards + mate) * count
        copies = [pltpu.make_async_copy(blocks_ref.at[colour], own_buf, sems.at[0])]
        for n, (_, start, height, _) in enumerate(places):
            long = height * stored * size
            src, dst = pieces[n].at[start:start + long], mate_buf.at[n * long:(n + 1) * long]
            copies.append(pltpu.make_async_copy(src, dst, sems.at[1 + n]))
        for c in copies:
            c.start()
        acc[...] = jnp.zeros_like(acc)
        for c in copies:
            c.wait()
        for n, (_, _, height, mask) in enumerate(places):
            first = lax.rem(band ^ mask, count // height) * height
            for i in range(height):
                a = first + i
                for k in range(stored):
                    at = ((n * height + i) * stored + k) * size
                    acc[cols_ref[(mate_at + a) * stored + k], a] += mate_buf[at:at + size].T

        def own(a, carry):
            for k in range(stored):
                acc[a, cols_ref[(own_at + a) * stored + k]] += own_buf[a, k]
            return carry

        lax.fori_loop(0, count, own, 0)
        write_parts(acc, hi_ref, lo_ref)

    return call(
        token, kernel, [cols, partners, blocks, *[in_hbm(p[0]) for p in places]],
        [SMEM, SMEM, HBM] + [HBM] * len(places),
        [VMEM, VMEM], [jax.ShapeDtypeStruct((rows, rows), bf16)] * 2,
        [
            pltpu.VMEM((count, stored, size, size), f32),
            pltpu.VMEM((count * stored * size, size), f32),
            pltpu.VMEM((count, count, size, size), f32),
            pltpu.SemaphoreType.DMA((1 + len(places),)),
        ],
        "build_couple",
    )


def scales(bounds_ref, step, shape):
    lowest, lower, upper = (jnp.full(shape, bounds_ref[i], f32) for i in range(3))
    half_width = (upper - lower) / 2.0
    centre = (upper + lower) / 2.0
    sigma_one = half_width / (lowest - centre)
    sigma_two = 1.0 / (2.0 / sigma_one - sigma_one)
    if step == 1:
        return sigma_one / half_width, None
    return 2.0 * sigma_two / half_width, -sigma_one * sigma_two


def apply_kernel(counts, step, has_partial, base_count, column, bounds_ref, *refs):
    refs = list(refs)
    mats = []
    for chunks in counts:
        hi, lo = refs.pop(0), refs.pop(0)
        mats.append((hi, lo, [refs.pop(0) for _ in range(chunks)]))
    partial = refs.pop(0) if has_partial else None
    base = [refs.pop(0) for _ in range(base_count)]
    if column is not None and column > 0:
        refs.pop(0)
    out_ref, w_buf, acc, sems = refs
    rows, width = acc.shape
    tiles = 1 if column is None else 4
    height = rows // tiles
    if step is not None:
        s_sum, s_base = scales(bounds_ref, step, (1, width))
    for m, (_, _, chunks) in enumerate(mats):
        at = 0
        for chunk in chunks:
            u_hi, u_lo = split(chunk[...])
            w_buf[m, at:at + chunk.shape[0], :width] = u_hi
            w_buf[m, at:at + chunk.shape[0], width:] = u_lo
            at += chunk.shape[0]
    copies = []
    for t in range(tiles):
        tile = slice(t * height, (t + 1) * height)
        for m, (hi, lo, _) in enumerate(mats):
            both = dot(hi[tile], w_buf[m])
            part = both[:, :width] + both[:, width:] + dot(lo[tile], w_buf[m, :, :width])
            if m == 0:
                acc[tile] = part
            else:
                acc[tile] += part
        result = acc[tile]
        if step is not None:
            result = result * s_sum
        if partial is not None:
            result = result + partial[tile]
        for chunk in base:
            result = result + chunk[tile] * s_base
        if column is None:
            out_ref[tile] = result
        else:
            acc[tile] = result
            dst = out_ref.at[tile, column:column + width]
            copies.append(pltpu.make_async_copy(acc.at[tile], dst, sems.at[t]))
            copies[-1].start()
    for c in copies:
        c.wait()


def apply(
    token, bounds, mats, step=None, partial=None, base=(), column=None, out_width=None, into=None,
    waits=(), last=False,
):
    rows = mats[0][0].shape[0]
    width = mats[0][2][0].shape[1]
    operands = [bounds]
    specs = [SMEM]
    for hi, lo, chunks in mats:
        operands += [hi, lo, *chunks]
        specs += [VMEM] * (2 + len(chunks))
    if partial is not None:
        operands.append(partial)
        specs.append(VMEM)
    operands += list(base)
    specs += [VMEM] * len(base)
    aliases = {}
    if into is not None:
        aliases = {len(operands): 0}
        operands.append(into)
        specs.append(HBM)
    shape = array(rows, width if column is None else out_width)
    kernel = functools.partial(
        apply_kernel, [len(m[2]) for m in mats], step, partial is not None, len(base), column
    )
    (out,), token = call(
        token, kernel, operands, specs, [VMEM if column is None else HBM], [shape],
        [
            pltpu.VMEM((len(mats), rows, 2 * width), bf16),
            pltpu.VMEM((rows, width), f32),
            pltpu.SemaphoreType.DMA((8,)),
        ],
        "apply", aliases, waits, last,
    )
    return out, token


def gate(x, *after):
    return lax.optimization_barrier((x, *after))[0]


def local(
    n_rows, n_bands,
    vectors, local_blocks, local_cols, coupling_blocks, coupling_cols, partners, bounds, rotation
):
    rows, band = vectors.shape
    colours, block_count = coupling_blocks.shape[:2]
    half = band // 2
    bits = n_rows.bit_length() - 1
    by_bit = bits == colours
    slots = range(colours)

    def to_band(x, mask):
        return lax.ppermute(x, "bands", [(i, i ^ mask) for i in range(n_bands)])

    def to_row(x, bit):
        return lax.ppermute(x, "rows", [(i, i ^ (1 << bit)) for i in range(n_rows)])

    def exchange(x, slot):
        if by_bit:
            return to_row(x, slot)
        taken = jnp.zeros_like(x)
        for bit in range(bits):
            taken = jnp.where(partners[slot, 0] == (1 << bit), to_row(x, bit), taken)
        return taken

    blocks = in_hbm(coupling_blocks)
    spin = in_hbm(rotation)
    flat_cols = coupling_cols.reshape(-1)
    token = jnp.zeros((8, 128), f32)

    chip_mate = to_band(vectors, 1)

    masks = list(range(2, n_bands, 2))
    order = list(slots)[::-1]
    near = [k for k in slots if by_bit and k == 0]
    far = [k for k in slots if k not in near]
    heights = [block_count // (2 if k in near else n_bands) for k in slots]
    stored = coupling_blocks.shape[2]
    vecs = in_hbm(vectors)
    part, mate_r, shares, token = begin(token, vecs, spin, partners, blocks, masks, heights, by_bit)
    sent, token = rotate_first(token, part, chip_mate, mate_r, len(masks))
    came = [to_band(c, mask) for c, mask in zip(sent, masks)]
    second, own_first, own_second, token = rotate_rest(token, vecs, chip_mate, spin, masks)
    shares = [s.reshape(-1, s.shape[-1]) for s in shares]
    shares = {k: exchange(gate(shares[k], token) if k in near else shares[k], k) for k in order}
    (total, joined), token = meet(token, [own_first, *came], [shares[k] for k in far])
    later = [to_band(gate(c, token), mask) for c, mask in zip(second, masks)]
    field = [total]
    passed = [to_band(joined, mask) for mask in masks]

    def send(part, after=None):
        return {k: exchange(gate(part, after) if k in near and after is not None else part, k) for k in order}

    def part_sum(terms, *rest, **options):
        nonlocal token
        out, token = apply(token, bounds, terms, *rest, **options)
        return out

    (total,), token = meet(token, [own_second, *later], (), [shares[k] for k in near])
    field.append(total)
    arrived = [send(field[0], token)]
    local_parts, token = build_local(token, local_blocks, local_cols.reshape(-1), bounds)
    waits = []
    partial = [part_sum([(*local_parts, [field[0]])], 1, waits=waits)]
    token = touch(token, [arrived[0][k] for k in slots])

    total = gate(total, token)
    arrived.append({k: exchange(total, k) for k in far})

    held = {}
    for mask, x in zip([0, *masks], [joined, *passed]):
        held[mask] = gate(x, token)
        held[mask ^ 1] = to_band(held[mask], 1)
    for k in near:
        shares[k] = gate(shares[k], token)
    size = coupling_blocks.shape[-1]
    mats = {}
    for k in far + near:
        if k in near:
            places = [(shares[k], 0, heights[k], 0), (to_band(shares[k], 1), 0, heights[k], 1)]
        else:
            at = far.index(k) * heights[k] * stored * size
            places = [(x, at, heights[k], m) for m, x in held.items()]
        mats[k], token = build_couple(token, k, by_bit, flat_cols, partners, blocks, places)
        if k == far[0] and near:
            arrived[1].update({n: exchange(gate(total, token), n) for n in near})
    first = []
    for h in range(2):
        if h == 1:
            partial.append(part_sum([(*local_parts, [field[1]])], 1))
        terms = [(*mats[k], [arrived[h][k]]) for k in slots]
        first.append(part_sum(terms, 1, partial[h]))
    arrived = [send(f) for f in first]
    out = None
    for h in range(2):
        terms = [(*local_parts, [first[h]])] + [(*mats[k], [arrived[h][k]]) for k in near]
        early = part_sum(terms, 2, None, [field[h]])
        for k in far[:-1]:
            early = part_sum([(*mats[k], [arrived[h][k]])], 2, early)
        k = far[-1]
        out = part_sum([(*mats[k], [arrived[h][k]])], 2, early, (), h * half, band, out, last=h == 1)
    return out


def solution(mesh):
    in_specs = (
        P("rows", "bands"),
        P("rows", None, None, None),
        P("rows", None),
        P(None, "rows", None, None, None),
        P(),
        P(),
        P(),
        P(),
    )
    body = functools.partial(local, mesh.shape["rows"], mesh.shape["bands"])
    return jax.shard_map(
        body, mesh=mesh, in_specs=in_specs, out_specs=P("rows", "bands"), check_vma=False
    )
```
